256 devices in a mesh: seq: 64 (over z, y, core), grp: 4 (over x).
Axes of the slice: x: 4, y: 4, z: 8, core: 2. Of those that a mesh axis runs over, the one named last changes fastest.
Arguments:
- queries: bfloat16 [4, 8192, 8192], P('grp', 'seq'), may hold values from -6 to 6
- keys_values: bfloat16 [2, 64, 128, 8192], P(None, 'seq', 'grp'), may hold values from -6 to 6
- neighbours: int32 [4, 128, 2], P('grp'), may hold values from 0 to 63, all different within a row
- grad_context: bfloat16 [4, 8192, 8192], P('grp', 'seq'), may hold values from -6 to 6
Outputs:
- context: bfloat16 [4, 8192, 8192], P('grp', 'seq')
- d_queries: bfloat16 [4, 8192, 8192], P('grp', 'seq')
- d_keys_values: bfloat16 [2, 64, 128, 8192], P(None, 'seq', 'grp')
The draws below stay inside these ranges and needn't reach their ends.
Inputs may be any that keep to these rules, and one draw needn't show every extreme that they name: `neighbours`: the 2 blocks of one span differ, and every block is retrieved by some span.
All inputs are finite; a program needn't handle non-finite values.
Results may differ from the reference program's by a relative error of at most 0.015.
Values may be sent and summed in bfloat16 or wider, within the bound.
A program may use at most 128 MiB of HBM per device.

```python
import math
import jax
import jax.numpy as jnp
from jax import lax

HEAD_DIM = 128
SPAN = 64
NBR = 2
ROWS = 128
HEADS = 64
HD = 8192
LENGTH = 8192
SPANS = 128
NBLK = 64
SEQS = 4


def draw_queries(key, part):
    key = jax.random.fold_in(key, 11)
    samples = jnp.clip(jax.random.normal(key, (SEQS, LENGTH, HD), jnp.float32), -6.0, 6.0)
    return samples.astype(jnp.bfloat16)


def draw_keys_values(key, part):
    key = jax.random.fold_in(key, 23)
    samples = jnp.clip(jax.random.normal(key, (2, NBLK, ROWS, HD), jnp.float32), -6.0, 6.0)
    return samples.astype(jnp.bfloat16)


def levels(key, dims, cuts, low, high):
    loudness = 1.0
    for dim, parts in cuts:
        heights = jax.random.uniform(jax.random.fold_in(jax.random.fold_in(key, 6), dim), (parts,), jnp.float32, low / len(cuts), high / len(cuts))
        loudness = loudness * jnp.repeat(jnp.exp(heights), dims[dim] // parts).reshape((-1,) + (1,) * (len(dims) - 1 - dim))
    return loudness


def choose_distinct(stream_key, rows, count, top, lift):
    ranking = jax.random.permutation(jax.random.fold_in(stream_key, 1), count)
    pull = ranking
    for power in range(3):
        pull = pull * pull // count
    pull = pull * lift // count
    lots = jax.random.randint(jax.random.fold_in(stream_key, 2), (rows, count), 0, 4096) + pull
    holders = jax.random.permutation(jax.random.fold_in(stream_key, 3), rows)[jnp.arange(count) % rows]
    lots = jnp.where(jnp.arange(rows)[:, None] == holders[None, :], 1 << 14, lots)
    merit = lots * count + jnp.arange(count)
    return lax.top_k(merit.astype(jnp.int32), top)[1].astype(jnp.int32)


def noise(stream_key, extent, width, limit, cuts=(), held_as=jnp.bfloat16):
    values = jax.random.normal(stream_key, extent, jnp.float32) * width
    if len(cuts) > 0:
        values = levels(stream_key, extent, cuts, -0.22, 0.18) * values
    return jnp.clip(values, min=-limit, max=limit).astype(held_as)


def setup_inputs(seed: int = 0) -> dict:
    seeds = jax.random.split(jax.random.key(seed), 5)
    queries = draw_queries(jax.random.fold_in(seeds[4], 71), 0)
    keys_values = draw_keys_values(jax.random.fold_in(seeds[4], 71), 0)
    neighbours = choose_distinct(seeds[2], SEQS * SPANS, NBLK, NBR, 512).reshape((SEQS, SPANS, NBR))
    grad_context = noise(seeds[3], (SEQS, LENGTH, HD), 1.0, 6.0, ((0, 4), (1, 64)))
    return {"queries": queries, "keys_values": keys_values, "neighbours": neighbours, "grad_context": grad_context}


exact_mode = lax.Precision.HIGHEST

def sequence_pass(query_seq, keyval_head, cotangent_seq, span_links):
    length = query_seq.shape[0]
    head_dim = query_seq.shape[1]
    margin = SPAN - 1
    blocks_all = keyval_head.shape[1]
    rows_block = keyval_head.shape[2]
    num_spans = length // SPAN
    per_step = min(num_spans, max(1, 2048 // SPAN))
    step_count = num_spans // per_step
    scaling = 1.0 / math.sqrt(head_dim)
    pad_rows = jnp.zeros((margin, head_dim), jnp.bfloat16)
    shifted_query = jnp.concatenate([query_seq[margin:], pad_rows], 0).reshape(step_count, per_step, SPAN, head_dim)
    shifted_grad = jnp.concatenate([cotangent_seq[margin:], pad_rows], 0).reshape(step_count, per_step, SPAN, head_dim)
    links = span_links.reshape(step_count, per_step, NBR)

    def one_step(grad_blocks, pieces):
        query_block, grad_block, link_block = pieces
        key_rows = keyval_head[0][link_block].reshape(per_step, NBR * rows_block, head_dim).astype(jnp.float32)
        value_rows = keyval_head[1][link_block].reshape(per_step, NBR * rows_block, head_dim).astype(jnp.float32)
        query_wide = query_block.astype(jnp.float32)
        grad_wide = grad_block.astype(jnp.float32)
        scores = jnp.einsum('cqd,ckd->cqk', query_wide, key_rows, precision=exact_mode) * scaling
        largest = lax.optimization_barrier(jnp.max(scores, axis=-1, keepdims=True))
        exponent = jnp.exp(scores - largest)
        weights = exponent / lax.optimization_barrier(jnp.sum(exponent, axis=-1, keepdims=True))
        weights_low = lax.optimization_barrier(weights.astype(jnp.bfloat16)).astype(jnp.float32)
        attended = jnp.einsum('cqk,ckd->cqd', weights_low, value_rows, precision=exact_mode).astype(jnp.bfloat16)
        grad_weights = jnp.einsum('cqd,ckd->cqk', grad_wide, value_rows, precision=exact_mode)
        row_total = lax.optimization_barrier(jnp.sum(grad_weights * weights, axis=-1, keepdims=True))
        grad_scores = lax.optimization_barrier((weights * (grad_weights - row_total) * scaling).astype(jnp.bfloat16)).astype(jnp.float32)
        grad_query = jnp.einsum('cqk,ckd->cqd', grad_scores, key_rows, precision=exact_mode).astype(jnp.bfloat16)
        grad_keys = jnp.einsum('cqk,cqd->ckd', grad_scores, query_wide, precision=exact_mode)
        grad_values = jnp.einsum('cqk,cqd->ckd', weights_low, grad_wide, precision=exact_mode)
        flat_links = link_block.reshape(-1).astype(jnp.int32)
        summed_keys = jax.ops.segment_sum(grad_keys.reshape(per_step * NBR, rows_block, head_dim), flat_links, num_segments=blocks_all)
        summed_values = jax.ops.segment_sum(grad_values.reshape(per_step * NBR, rows_block, head_dim), flat_links, num_segments=blocks_all)
        grad_blocks = grad_blocks + jnp.stack([summed_keys, summed_values])
        return (grad_blocks, (attended, grad_query))
    start_grad = jnp.zeros((2, blocks_all, rows_block, head_dim), jnp.float32)
    grad_blocks, (attended, grad_query) = lax.scan(one_step, start_grad, (shifted_query, shifted_grad, links))
    attended = attended.reshape(length, head_dim)
    grad_query = grad_query.reshape(length, head_dim)
    context = jnp.concatenate([pad_rows, attended[:length - margin]], 0)
    query_back = jnp.concatenate([pad_rows, grad_query[:length - margin]], 0)
    return (context, query_back, grad_blocks)

def reference(queries, keys_values, neighbours, grad_context):

    def per_head(offset):
        query_head = lax.dynamic_slice_in_dim(queries, offset, HEAD_DIM, 2)
        cotan_head = lax.dynamic_slice_in_dim(grad_context, offset, HEAD_DIM, 2)
        keyval_head = lax.dynamic_slice_in_dim(keys_values, offset, HEAD_DIM, 3)
        contexts = []
        query_grads = []
        total_grad = jnp.zeros((2, NBLK, ROWS, HEAD_DIM), jnp.float32)
        for member in range(SEQS):
            context, query_back, grad_blocks = sequence_pass(query_head[member], keyval_head, cotan_head[member], neighbours[member])
            contexts.append(context)
            query_grads.append(query_back)
            total_grad = total_grad + grad_blocks
        return (jnp.stack(contexts), jnp.stack(query_grads), total_grad)
    offsets = jnp.arange(HEADS, dtype=jnp.int32) * HEAD_DIM
    context_all, grad_all, block_all = lax.map(per_head, offsets)
    context = jnp.transpose(context_all, (1, 2, 0, 3)).reshape(SEQS, LENGTH, HEADS * HEAD_DIM)
    d_queries = jnp.transpose(grad_all, (1, 2, 0, 3)).reshape(SEQS, LENGTH, HEADS * HEAD_DIM)
    d_keys_values = jnp.transpose(block_all, (1, 2, 3, 0, 4)).reshape(2, NBLK, ROWS, HEADS * HEAD_DIM).astype(jnp.bfloat16)
    return (context, d_queries, d_keys_values)
```

```python
import functools
import math

import jax
import jax.numpy as jnp
from jax import lax
from jax.experimental import pallas as pl
from jax.experimental.pallas import tpu as pltpu
from jax.sharding import PartitionSpec as P

SPAN = 64
NBR = 2
HEAD = 128
PLANE = 8
MESH = pl.DeviceIdType.MESH
BF16 = jnp.bfloat16
F32 = jnp.float32


def dot_nt(a, b):
    return lax.dot_general(a, b, (((1,), (1,)), ((), ())), preferred_element_type=F32)


def dot_nn(a, b):
    return lax.dot_general(a, b, (((1,), (0,)), ((), ())), preferred_element_type=F32)


def dot_tn(a, b):
    return lax.dot_general(a, b, (((0,), (0,)), ((), ())), preferred_element_type=F32)


def kernel(nz, nx, meta, q_in, kv_in, g_in, ctx_out, dq_out, dkv_out,
           kv_a, kv_b, q_a, q_b, g_a, g_b, ctx_a, ctx_b, dq_a, dq_b,
           sum_k, sum_v, part_a, part_b, half_a, half_b, full_a, full_b,
           own_a, own_b, roll_c, roll_d,
           in_send, in_recv, ag_send, ag_recv, rs_send, rs_recv, out_send, out_recv):
    np_ = nx * PLANE
    tokens = q_in.shape[1]
    rows = kv_in.shape[2]
    spans = PLANE * tokens // SPAN + 1
    slots = spans * nx * NBR
    far = nz // 2
    scaling = 1.0 / math.sqrt(HEAD)
    seq = lax.axis_index("seq")
    x = lax.axis_index("grp")
    z = seq // PLANE
    yc = seq % PLANE
    me = x * PLANE + yc
    kv = (kv_a, kv_b)
    q = (q_a, q_b)
    g = (g_a, g_b)
    ctx = (ctx_a, ctx_b)
    dq = (dq_a, dq_b)
    part = (part_a, part_b)
    half = (half_a, half_b)
    full = (full_a, full_b)
    own = (own_a, own_b)

    def zone(zz):
        return pl.ds(pl.multiple_of(zz * PLANE, PLANE), PLANE)

    def near(offset):
        return (z + offset + nz) % nz

    def z_device(offset):
        return (near(offset) * PLANE + yc, x)

    def peer(r):
        m = (me + r) % np_
        return m, m // PLANE, m % PLANE

    def columns(m, h):
        return pl.ds(pl.multiple_of((m * 2 + h) * HEAD, HEAD), HEAD)

    zero_rows = jnp.zeros((nx, SPAN, HEAD), BF16)
    for h in range(2):
        for buf in (q[h], g[h]):
            buf[:, :16, :] = jnp.zeros((nx, 16, HEAD), BF16)
            buf[:, 16 + PLANE * tokens:, :] = zero_rows
    sum_k[0] = jnp.zeros((HEAD, HEAD), F32)
    sum_v[0] = jnp.zeros((HEAD, HEAD), F32)

    barrier = pltpu.get_barrier_semaphore()

    def greet(r, carry):
        m, px, pyc = peer(r)
        pl.semaphore_signal(barrier, inc=1, device_id=(z * PLANE + pyc, px), device_id_type=MESH)
        return carry

    lax.fori_loop(1, np_, greet, 0)
    for offset in (-1, 1):
        pl.semaphore_signal(barrier, inc=1, device_id=z_device(offset), device_id_type=MESH)
    pl.semaphore_wait(barrier, np_ + 1)

    def tok_rows(k):
        return pl.ds(pl.multiple_of(16 + k * tokens, 16), tokens)

    def blk_rows(k):
        return pl.ds(pl.multiple_of(k * rows, rows), rows)

    def kv_dst(h):
        return kv[h].at[:, seq, blk_rows(x), :]

    def q_dst(buf):
        return buf.at[x, tok_rows(yc), :]

    def send_kv(h):
        def body(r, carry):
            m, px, pyc = peer(r)
            pltpu.make_async_remote_copy(
                src_ref=kv_in.at[:, 0, :, columns(m, h)], dst_ref=kv_dst(h),
                send_sem=in_send.at[h], recv_sem=in_recv.at[h],
                device_id=(z * PLANE + pyc, px), device_id_type=MESH).start()
            return carry
        pltpu.make_async_copy(kv_in.at[:, 0, :, columns(me, h)], kv_dst(h), in_recv.at[h]).start()
        lax.fori_loop(1, np_, body, 0)

    def send_qg(h):
        def body(r, carry):
            m, px, pyc = peer(r)
            for k, (src, dst) in enumerate(((q_in, q[h]), (g_in, g[h]))):
                sem = 2 + 2 * k + h
                pltpu.make_async_remote_copy(
                    src_ref=src.at[0, :, columns(m, h)], dst_ref=q_dst(dst),
                    send_sem=in_send.at[sem], recv_sem=in_recv.at[sem],
                    device_id=(z * PLANE + pyc, px), device_id_type=MESH).start()
            return carry
        for k, (src, dst) in enumerate(((q_in, q[h]), (g_in, g[h]))):
            pltpu.make_async_copy(
                src.at[0, :, columns(me, h)], q_dst(dst), in_recv.at[2 + 2 * k + h]).start()
        lax.fori_loop(1, np_, body, 0)

    def wait_bytes(ref, sem):
        pltpu.make_async_copy(ref, ref, sem).wait()

    def wait_kv(h):
        wait_bytes(kv[h].at[:, zone(z)], in_recv.at[h])

    def wait_qg(h):
        for k, buf in enumerate((q[h], g[h])):
            wait_bytes(buf.at[:, pl.ds(16, PLANE * tokens), :], in_recv.at[2 + 2 * k + h])

    def wait_in_sends():
        for h in range(2):
            wait_bytes(kv_in.at[:, 0, :, pl.ds(0, (np_ - 1) * HEAD)], in_send.at[h])
            for k, src in enumerate((q_in, g_in)):
                wait_bytes(src.at[0, :, pl.ds(0, (np_ - 1) * HEAD)], in_send.at[2 + 2 * k + h])

    def ag_copy(h, way, step, kind):
        sign = 1 - 2 * way
        part_ref = kv[h].at[kind, zone(near(-sign * (step - 1)))]
        return pltpu.make_async_remote_copy(
            src_ref=part_ref, dst_ref=part_ref,
            send_sem=ag_send.at[h, way, step - 1, kind], recv_sem=ag_recv.at[h, way, step - 1, kind],
            device_id=z_device(sign), device_id_type=MESH)

    def ag_has(way, step, kind):
        return step < far or kind == way

    def ag_start(h, step, kind):
        for way in range(2):
            if ag_has(way, step, kind):
                ag_copy(h, way, step, kind).start()

    def ag_wait(h, way, step, kind):
        sign = 1 - 2 * way
        wait_bytes(kv[h].at[kind, zone(near(-sign * step))], ag_recv.at[h, way, step - 1, kind])

    def ag_forward(h, step, kind):
        for way in range(2):
            ag_wait(h, way, step - 1, kind)
            if ag_has(way, step, kind):
                ag_copy(h, way, step, kind).start()

    def ag_last(h):
        for kind in range(2):
            for way in range(2):
                if ag_has(way, far, kind):
                    ag_wait(h, way, far, kind)

    def rs_send_step(h, step):
        for way in range(2):
            sign = 1 - 2 * way
            zz = zone(near(sign * (far + 1 - step)))
            if step == 1:
                src, dst = part[h].at[way, zz], half[h].at[way]
            else:
                src, dst = part[h].at[:, zz], full[h].at[way, step - 2]
            pltpu.make_async_remote_copy(
                src_ref=src, dst_ref=dst,
                send_sem=rs_send.at[h, way, step - 1], recv_sem=rs_recv.at[h, way, step - 1],
                device_id=z_device(sign), device_id_type=MESH).start()

    def rs_wait(h, way, step):
        ref = half[h].at[way] if step == 1 else full[h].at[way, step - 2]
        wait_bytes(ref, rs_recv.at[h, way, step - 1])

    def rs_step(h, step):
        for way in range(2):
            sign = 1 - 2 * way
            base = near(sign * (far + 1 - step)) * PLANE
            rs_wait(h, way, step - 1)

            def add(b, carry):
                if step == 2:
                    part[h][way, base + b] = (
                        part[h][way, base + b].astype(F32) + half[h][way, b].astype(F32)).astype(BF16)
                else:
                    for kind in range(2):
                        part[h][kind, base + b] = (
                            part[h][kind, base + b].astype(F32)
                            + full[h][way, step - 3, kind, b].astype(F32)).astype(BF16)
                return carry

            lax.fori_loop(0, PLANE, add, 0)
        rs_send_step(h, step)

    def rs_last(h):
        for way in range(2):
            rs_wait(h, way, far)

        def add(b, carry):
            for kind in range(2):
                total = part[h][kind, z * PLANE + b].astype(F32)
                for way in range(2):
                    if far > 1:
                        total += full[h][way, far - 2, kind, b].astype(F32)
                    elif kind == way:
                        total += half[h][way, b].astype(F32)
                own[h][kind, b] = total.astype(BF16)
            return carry

        lax.fori_loop(0, PLANE, add, 0)

        def body(r, carry):
            m, px, pyc = peer(r)
            pltpu.make_async_remote_copy(
                src_ref=own[h].at[:, pyc, blk_rows(px), :], dst_ref=dkv_out.at[:, 0, :, columns(me, h)],
                send_sem=out_send.at[h], recv_sem=out_recv.at[0],
                device_id=(z * PLANE + pyc, px), device_id_type=MESH).start()
            return carry

        pltpu.make_async_copy(
            own[h].at[:, yc, blk_rows(x), :], dkv_out.at[:, 0, :, columns(me, h)], out_recv.at[0]).start()
        lax.fori_loop(1, np_, body, 0)

    def out_rows(k):
        return pl.ds(pl.multiple_of(SPAN + k * tokens, 16), tokens)

    def send_out(h):
        def body(r, carry):
            m, px, pyc = peer(r)
            for k, (src, dst) in enumerate(((ctx[h], ctx_out), (dq[h], dq_out))):
                pltpu.make_async_remote_copy(
                    src_ref=src.at[px, out_rows(pyc), :], dst_ref=dst.at[0, :, columns(me, h)],
                    send_sem=out_send.at[2 + 2 * k + h], recv_sem=out_recv.at[1 + k],
                    device_id=(z * PLANE + pyc, px), device_id_type=MESH).start()
            return carry
        for k, (src, dst) in enumerate(((ctx[h], ctx_out), (dq[h], dq_out))):
            pltpu.make_async_copy(
                src.at[x, out_rows(yc), :], dst.at[0, :, columns(me, h)], out_recv.at[1 + k]).start()
        lax.fori_loop(1, np_, body, 0)

    def compute(h, events):
        row_id = lax.broadcasted_iota(jnp.int32, (SPAN, HEAD), 0)

        def shifted(buf, s, v):
            wide = buf[s, pl.ds(pl.multiple_of(v * SPAN, SPAN), SPAN + 16), :].astype(F32)
            return pltpu.roll(wide, SPAN + 1, 0)[:SPAN].astype(BF16)

        def store_back(out, hold, s, v, value):
            rolled = pltpu.roll(value, SPAN - 1, 0)
            out[s, pl.ds(pl.multiple_of(v * SPAN, SPAN), SPAN), :] = jnp.where(
                row_id == SPAN - 1, rolled, hold[s]).astype(BF16)
            hold[s] = rolled

        def step(v, carry):
            head_start = jnp.logical_and(z == 0, v == 0)
            keep = jnp.where(head_start, 0.0, 1.0)
            for s in range(nx):
                slot = (v * nx + s) * NBR
                qs = shifted(q[h], s, v)
                gs = (shifted(g[h], s, v).astype(F32) * keep).astype(BF16)
                link = [meta[slot + j] for j in range(NBR)]
                keys = jnp.concatenate([kv[h][0, link[j]] for j in range(NBR)], 0)
                vals = jnp.concatenate([kv[h][1, link[j]] for j in range(NBR)], 0)
                scores = dot_nt(qs, keys)
                grad_w = dot_nt(gs, vals)
                largest = jnp.max(scores, axis=-1, keepdims=True)
                expo = jnp.exp2((scores - largest) * (scaling * math.log2(math.e)))
                weights = expo * (1.0 / jnp.sum(expo, axis=-1, keepdims=True))
                low = weights.astype(BF16)
                total = jnp.sum(grad_w * weights, axis=-1, keepdims=True)
                grad_s = (weights * (grad_w - total) * scaling).astype(BF16)
                store_back(ctx[h], roll_c, s, v, dot_nn(low, vals) * keep)
                store_back(dq[h], roll_d, s, v, dot_nn(grad_s, keys))
                grad_k = dot_tn(grad_s, qs)
                grad_v = dot_tn(low, gs)
                for j in range(NBR):
                    before = meta[slots + slot + j]
                    cut = slice(j * HEAD, (j + 1) * HEAD)
                    sum_k[slot + j + 1] = sum_k[before] + grad_k[cut]
                    sum_v[slot + j + 1] = sum_v[before] + grad_v[cut]
            for when, event in events:
                pl.when(v == min(when, spans - 1))(event)
            return carry

        lax.fori_loop(0, spans, step, 0)

        def gather(b, carry):
            last = meta[2 * slots + b]
            part[h][0, b] = sum_k[last].astype(BF16)
            part[h][1, b] = sum_v[last].astype(BF16)
            return carry

        lax.fori_loop(0, nz * PLANE, gather, 0)

    send_kv(0)
    send_kv(1)
    send_qg(0)
    wait_kv(0)
    for kind in range(2):
        ag_start(0, 1, kind)
    send_qg(1)
    for step in range(2, far + 1):
        for kind in range(2):
            ag_forward(0, step, kind)
    wait_kv(1)
    for kind in range(2):
        ag_start(1, 1, kind)
    ag_last(0)
    wait_qg(0)
    events = []
    at = [4, 7, 11, 14, 16, 16]
    for step in range(2, far + 1):
        for kind in range(2):
            events.append((at[len(events)], functools.partial(ag_forward, 1, step, kind)))
    compute(0, events)
    rs_send_step(0, 1)
    send_out(0)
    ag_last(1)
    wait_qg(1)
    events = []
    at = [3, 8, 14]
    for step in range(2, far + 1):
        events.append((at[len(events)], functools.partial(rs_step, 0, step)))
    compute(1, events)
    rs_send_step(1, 1)
    send_out(1)
    rs_last(0)
    for step in range(2, far + 1):
        rs_step(1, step)
    rs_last(1)

    wait_in_sends()
    for h in range(2):
        for way in range(2):
            for step in range(1, far + 1):
                for kind in range(2):
                    if ag_has(way, step, kind):
                        ag_copy(h, way, step, kind).wait_send()
                ref = half[h].at[way] if step == 1 else full[h].at[way, step - 2]
                wait_bytes(ref, rs_send.at[h, way, step - 1])
        wait_bytes(dkv_out.at[:, 0, :, pl.ds(0, (np_ - 1) * HEAD)], out_send.at[h])
        for k, dst in enumerate((ctx_out, dq_out)):
            wait_bytes(dst.at[0, :, pl.ds(0, (np_ - 1) * HEAD)], out_send.at[2 + 2 * k + h])
    for k, dst in enumerate((dkv_out, ctx_out, dq_out)):
        wait_bytes(dst, out_recv.at[k])


def make_meta(neighbours, nz, nx):
    nblk = nz * PLANE
    z = lax.axis_index("seq") // PLANE
    links = lax.all_gather(neighbours[0], "grp", axis=0, tiled=False)
    per_plane = links.shape[1] // nz
    links = jnp.concatenate([jnp.zeros((nx, 1, NBR), jnp.int32), links], 1)
    links = lax.dynamic_slice_in_dim(links, z * per_plane, per_plane + 1, 1)
    links = jnp.transpose(links, (1, 0, 2)).reshape(-1)
    n = links.shape[0]
    ids = jnp.arange(n, dtype=jnp.int32)
    same = (links[:, None] == links[None, :]) & (ids[None, :] < ids[:, None])
    before = jnp.max(jnp.where(same, ids[None, :] + 1, 0), axis=1)
    here = links[None, :] == jnp.arange(nblk, dtype=jnp.int32)[:, None]
    last = jnp.max(jnp.where(here, ids[None, :] + 1, 0), axis=1)
    return jnp.concatenate([links, before, last])


def solution(mesh):
    nz = mesh.shape["seq"] // PLANE
    nx = mesh.shape["grp"]
    far = nz // 2

    def step(queries, keys_values, neighbours, grad_context):
        meta = make_meta(neighbours, nz, nx)
        tokens = queries.shape[1]
        nblk = nz * PLANE
        long_in = 16 + PLANE * tokens + SPAN
        long_out = PLANE * tokens + SPAN
        slots = (PLANE * tokens // SPAN + 1) * nx * NBR
        sem = pltpu.SemaphoreType.DMA
        twice = lambda shape: [pltpu.VMEM(shape, BF16)] * 2
        scratch = (
            twice((2, nblk, HEAD, HEAD))
            + twice((nx, long_in, HEAD)) + twice((nx, long_in, HEAD))
            + twice((nx, long_out, HEAD)) + twice((nx, long_out, HEAD))
            + [pltpu.VMEM((slots + 1, HEAD, HEAD), F32)] * 2
            + twice((2, nblk, HEAD, HEAD))
            + twice((2, PLANE, HEAD, HEAD))
            + twice((2, max(far - 1, 1), 2, PLANE, HEAD, HEAD))
            + twice((2, PLANE, HEAD, HEAD))
            + [pltpu.VMEM((nx, SPAN, HEAD), F32)] * 2
            + [sem((6,)), sem((6,)), sem((2, 2, far, 2)), sem((2, 2, far, 2)),
               sem((2, 2, far)), sem((2, 2, far)), sem((6,)), sem((3,))]
        )
        hbm = pl.BlockSpec(memory_space=pl.ANY)
        out = pl.pallas_call(
            functools.partial(kernel, nz, nx),
            out_shape=(
                jax.ShapeDtypeStruct(queries.shape, BF16),
                jax.ShapeDtypeStruct(queries.shape, BF16),
                jax.ShapeDtypeStruct(keys_values.shape, BF16),
            ),
            in_specs=[pl.BlockSpec(memory_space=pltpu.SMEM), hbm, hbm, hbm],
            out_specs=(hbm, hbm, hbm),
            scratch_shapes=scratch,
            compiler_params=pltpu.CompilerParams(
                collective_id=0, has_side_effects=True, vmem_limit_bytes=60 * 1024 * 1024
            ),
            name="plane_attention",
        )(meta, queries, keys_values, grad_context)
        return tuple(out)

    in_specs = (
        P("grp", "seq", None),
        P(None, "seq", "grp", None),
        P("grp", None, None),
        P("grp", "seq", None),
    )
    out_specs = (P("grp", "seq", None), P("grp", "seq", None), P(None, "seq", "grp", None))
    return jax.shard_map(step, mesh=mesh, in_specs=in_specs, out_specs=out_specs, check_vma=False)
```

```python
import functools
import math

import jax
import jax.numpy as jnp
from jax import lax
from jax.experimental import pallas as pl
from jax.experimental.pallas import tpu as pltpu
from jax.sharding import PartitionSpec as P

SPAN = 64
NBR = 2
HEAD = 128
AT_A0, AT_A1 = 6, 12
AT_B0, AT_B1, AT_B2 = 4, 9, 14
PLANE = 8
MESH = pl.DeviceIdType.MESH
BF16 = jnp.bfloat16
F32 = jnp.float32


def dot_nt(a, b):
    return lax.dot_general(a, b, (((1,), (1,)), ((), ())), preferred_element_type=F32)


def dot_nn(a, b):
    return lax.dot_general(a, b, (((1,), (0,)), ((), ())), preferred_element_type=F32)


def dot_tn(a, b):
    return lax.dot_general(a, b, (((0,), (0,)), ((), ())), preferred_element_type=F32)


def kernel(nz, nx, links_in, q_in, kv_in, g_in, ctx_out, dq_out, dkv_out,
           kv_a, kv_b, q_a, q_b, g_a, g_b, ctx_a, ctx_b, dq_a, dq_b,
           sum_k, sum_v, part_a, part_b, half_a, half_b, full_a, full_b,
           own_a, own_b, roll_c, roll_d, links, before_v, last_v, links_s, before_s, last_s,
           link_send, link_recv, in_send, in_recv, ag_send, ag_recv, rs_send, rs_recv, out_send, out_recv):
    np_ = nx * PLANE
    tokens = q_in.shape[1]
    rows = kv_in.shape[2]
    spans = PLANE * tokens // SPAN + 1
    far = nz // 2
    scaling = 1.0 / math.sqrt(HEAD)
    seq = lax.axis_index("seq")
    x = lax.axis_index("grp")
    z = seq // PLANE
    yc = seq % PLANE
    me = x * PLANE + yc
    kv = (kv_a, kv_b)
    q = (q_a, q_b)
    g = (g_a, g_b)
    ctx = (ctx_a, ctx_b)
    dq = (dq_a, dq_b)
    part = (part_a, part_b)
    half = (half_a, half_b)
    full = (full_a, full_b)
    own = (own_a, own_b)

    def zone(zz):
        return pl.ds(pl.multiple_of(zz * PLANE, PLANE), PLANE)

    def near(offset):
        return (z + offset + nz) % nz

    def z_device(offset):
        return (near(offset) * PLANE + yc, x)

    def peer(r):
        m = (me + r) % np_
        return m, m // PLANE, m % PLANE

    def columns(m, h):
        return pl.ds(pl.multiple_of((m * 2 + h) * HEAD, HEAD), HEAD)

    zero_rows = jnp.zeros((nx, SPAN, HEAD), BF16)
    for h in range(2):
        for buf in (q[h], g[h]):
            buf[:, :16, :] = jnp.zeros((nx, 16, HEAD), BF16)
            buf[:, 16 + PLANE * tokens:, :] = zero_rows
    sum_k[0] = jnp.zeros((HEAD, HEAD), F32)
    sum_v[0] = jnp.zeros((HEAD, HEAD), F32)

    barrier = pltpu.get_barrier_semaphore()

    def greet(r, carry):
        m, px, pyc = peer(r)
        pl.semaphore_signal(barrier, inc=1, device_id=(z * PLANE + pyc, px), device_id_type=MESH)
        return carry

    lax.fori_loop(1, np_, greet, 0)
    for offset in (-1, 1):
        pl.semaphore_signal(barrier, inc=1, device_id=z_device(offset), device_id_type=MESH)
    pl.semaphore_wait(barrier, np_ + 1)

    def tok_rows(k):
        return pl.ds(pl.multiple_of(16 + k * tokens, 16), tokens)

    def blk_rows(k):
        return pl.ds(pl.multiple_of(k * rows, rows), rows)

    def kv_dst(h):
        return kv[h].at[:, seq, blk_rows(x), :]

    def q_dst(buf):
        return buf.at[x, tok_rows(yc), :]

    def send_kv(h):
        def body(r, carry):
            m, px, pyc = peer(r)
            pltpu.make_async_remote_copy(
                src_ref=kv_in.at[:, 0, :, columns(m, h)], dst_ref=kv_dst(h),
                send_sem=in_send.at[h], recv_sem=in_recv.at[h],
                device_id=(z * PLANE + pyc, px), device_id_type=MESH).start()
            return carry
        pltpu.make_async_copy(kv_in.at[:, 0, :, columns(me, h)], kv_dst(h), in_recv.at[h]).start()
        lax.fori_loop(1, np_, body, 0)

    def send_qg(h):
        def body(r, carry):
            m, px, pyc = peer(r)
            for k, (src, dst) in enumerate(((q_in, q[h]), (g_in, g[h]))):
                sem = 2 + 2 * k + h
                pltpu.make_async_remote_copy(
                    src_ref=src.at[0, :, columns(m, h)], dst_ref=q_dst(dst),
                    send_sem=in_send.at[sem], recv_sem=in_recv.at[sem],
                    device_id=(z * PLANE + pyc, px), device_id_type=MESH).start()
            return carry
        for k, (src, dst) in enumerate(((q_in, q[h]), (g_in, g[h]))):
            pltpu.make_async_copy(
                src.at[0, :, columns(me, h)], q_dst(dst), in_recv.at[2 + 2 * k + h]).start()
        lax.fori_loop(1, np_, body, 0)

    def wait_bytes(ref, sem):
        pltpu.make_async_copy(ref, ref, sem).wait()

    def wait_kv(h):
        wait_bytes(kv[h].at[:, zone(z)], in_recv.at[h])

    def wait_qg(h):
        for k, buf in enumerate((q[h], g[h])):
            wait_bytes(buf.at[:, pl.ds(16, PLANE * tokens), :], in_recv.at[2 + 2 * k + h])

    def wait_in_sends():
        for h in range(2):
            wait_bytes(kv_in.at[:, 0, :, pl.ds(0, (np_ - 1) * HEAD)], in_send.at[h])
            for k, src in enumerate((q_in, g_in)):
                wait_bytes(src.at[0, :, pl.ds(0, (np_ - 1) * HEAD)], in_send.at[2 + 2 * k + h])

    def send_links():
        def body(r, carry):
            pltpu.make_async_remote_copy(
                src_ref=links_in, dst_ref=links.at[x], send_sem=link_send, recv_sem=link_recv.at[0],
                device_id=(seq, (x + r) % nx), device_id_type=MESH).start()
            return carry
        pltpu.make_async_copy(links_in, links.at[x], link_recv.at[0]).start()
        lax.fori_loop(1, nx, body, 0)

    def chain_links():
        wait_bytes(links, link_recv.at[0])
        copy = pltpu.make_async_copy(links, links_s, link_recv.at[1])
        copy.start()
        copy.wait()
        shape = links.shape[1:]
        row = lax.broadcasted_iota(jnp.int32, shape, 0)
        lane = lax.broadcasted_iota(jnp.int32, shape, 1)
        block = row * shape[1] + lane
        held = [links[s] for s in range(nx)]
        slot = [(lane * nx + s) * NBR + row + 1 for s in range(nx)]

        def body(v, carry):
            before, last = list(carry[:nx]), carry[nx]
            for s in range(nx):
                for j in range(NBR):
                    link = links_s[s, j, v]
                    here = (v * nx + s) * NBR + j + 1
                    for t in range(nx):
                        before[t] = jnp.where(
                            jnp.logical_and(held[t] == link, slot[t] > here), here, before[t])
                    last = jnp.where(block == link, here, last)
            return (*before, last)

        zero = jnp.zeros(shape, jnp.int32)
        found = lax.fori_loop(0, spans, body, (zero,) * (nx + 1))
        for s in range(nx):
            before_v[s] = found[s]
        last_v[...] = found[nx]
        copies = (pltpu.make_async_copy(before_v, before_s, link_recv.at[1]),
                  pltpu.make_async_copy(last_v, last_s, link_recv.at[2]))
        for copy in copies:
            copy.start()
        for copy in copies:
            copy.wait()

    def ag_copy(h, way, step, kind):
        sign = 1 - 2 * way
        part_ref = kv[h].at[kind, zone(near(-sign * (step - 1)))]
        return pltpu.make_async_remote_copy(
            src_ref=part_ref, dst_ref=part_ref,
            send_sem=ag_send.at[h, way, step - 1, kind], recv_sem=ag_recv.at[h, way, step - 1, kind],
            device_id=z_device(sign), device_id_type=MESH)

    def ag_has(way, step, kind):
        return step < far or kind == way

    def ag_start(h, step, turn):
        for way in range(2):
            kind = way if turn == 0 else 1 - way
            if ag_has(way, step, kind):
                ag_copy(h, way, step, kind).start()

    def ag_wait(h, way, step, kind):
        sign = 1 - 2 * way
        wait_bytes(kv[h].at[kind, zone(near(-sign * step))], ag_recv.at[h, way, step - 1, kind])

    def ag_forward(h, step, turn):
        for way in range(2):
            kind = way if turn == 0 else 1 - way
            ag_wait(h, way, step - 1, kind)
            if ag_has(way, step, kind):
                ag_copy(h, way, step, kind).start()

    def ag_last(h):
        for kind in range(2):
            for way in range(2):
                if ag_has(way, far, kind):
                    ag_wait(h, way, far, kind)

    def rs_has(way, step, kind):
        return step > 1 or kind == way

    def rs_dst(h, way, step, kind):
        return half[h].at[way] if step == 1 else full[h].at[way, step - 2, kind]

    def rs_base(way, step):
        return near((1 - 2 * way) * (far + 1 - step)) * PLANE

    def rs_send_part(h, way, step, kind):
        pltpu.make_async_remote_copy(
            src_ref=part[h].at[kind, pl.ds(pl.multiple_of(rs_base(way, step), PLANE), PLANE)],
            dst_ref=rs_dst(h, way, step, kind),
            send_sem=rs_send.at[h, way, step - 1, kind], recv_sem=rs_recv.at[h, way, step - 1, kind],
            device_id=z_device(1 - 2 * way), device_id_type=MESH).start()

    def rs_wait(h, way, step, kind):
        wait_bytes(rs_dst(h, way, step, kind), rs_recv.at[h, way, step - 1, kind])

    def rs_begin(h):
        for way in range(2):
            rs_send_part(h, way, 1, way)
        for way in range(2):
            if far > 1:
                rs_send_part(h, way, 2, 1 - way)

    def rs_step(h, step, turn):
        for way in range(2):
            kind = way if turn == 0 else 1 - way
            if not rs_has(way, step - 1, kind):
                continue
            base = rs_base(way, step)
            rs_wait(h, way, step - 1, kind)
            got = rs_dst(h, way, step - 1, kind)

            def add(b, carry):
                part[h][kind, base + b] = (
                    part[h][kind, base + b].astype(F32) + got[b].astype(F32)).astype(BF16)
                return carry

            lax.fori_loop(0, PLANE, add, 0)
            rs_send_part(h, way, step, kind)

    def rs_last(h):
        for kind in range(2):
            ways = [way for way in range(2) if rs_has(way, far, kind)]
            for way in ways:
                rs_wait(h, way, far, kind)

            def add(b, carry):
                total = part[h][kind, z * PLANE + b].astype(F32)
                for way in ways:
                    total += rs_dst(h, way, far, kind)[b].astype(F32)
                own[h][kind, b] = total.astype(BF16)
                return carry

            lax.fori_loop(0, PLANE, add, 0)

        def body(r, carry):
            m, px, pyc = peer(r)
            pltpu.make_async_remote_copy(
                src_ref=own[h].at[:, pyc, blk_rows(px), :], dst_ref=dkv_out.at[:, 0, :, columns(me, h)],
                send_sem=out_send.at[h], recv_sem=out_recv.at[0],
                device_id=(z * PLANE + pyc, px), device_id_type=MESH).start()
            return carry

        pltpu.make_async_copy(
            own[h].at[:, yc, blk_rows(x), :], dkv_out.at[:, 0, :, columns(me, h)], out_recv.at[0]).start()
        lax.fori_loop(1, np_, body, 0)

    def out_rows(k):
        return pl.ds(pl.multiple_of(SPAN + k * tokens, 16), tokens)

    def send_out(h):
        def body(r, carry):
            m, px, pyc = peer(r)
            for k, (src, dst) in enumerate(((ctx[h], ctx_out), (dq[h], dq_out))):
                pltpu.make_async_remote_copy(
                    src_ref=src.at[px, out_rows(pyc), :], dst_ref=dst.at[0, :, columns(me, h)],
                    send_sem=out_send.at[2 + 2 * k + h], recv_sem=out_recv.at[1 + k],
                    device_id=(z * PLANE + pyc, px), device_id_type=MESH).start()
            return carry
        for k, (src, dst) in enumerate(((ctx[h], ctx_out), (dq[h], dq_out))):
            pltpu.make_async_copy(
                src.at[x, out_rows(yc), :], dst.at[0, :, columns(me, h)], out_recv.at[1 + k]).start()
        lax.fori_loop(1, np_, body, 0)

    def compute(h, events):
        row_id = lax.broadcasted_iota(jnp.int32, (SPAN, HEAD), 0)

        def shifted(buf, s, v):
            wide = buf[s, pl.ds(pl.multiple_of(v * SPAN, SPAN), SPAN + 16), :].astype(F32)
            return pltpu.roll(wide, SPAN + 1, 0)[:SPAN]

        def store_back(out, hold, s, v, value):
            rolled = pltpu.roll(value, SPAN - 1, 0)
            out[s, pl.ds(pl.multiple_of(v * SPAN, SPAN), SPAN), :] = jnp.where(
                row_id == SPAN - 1, rolled, hold[s]).astype(BF16)
            hold[s] = rolled

        def step(v, carry):
            head_start = jnp.logical_and(z == 0, v == 0)
            keep = jnp.where(head_start, 0.0, 1.0)
            group = range(nx)
            slot = [(v * nx + s) * NBR for s in group]
            link = [[links_s[s, j, v] for j in range(NBR)] for s in group]
            qs = [shifted(q[h], s, v).astype(BF16) for s in group]
            gs = [(shifted(g[h], s, v) * keep).astype(BF16) for s in group]
            keys = [jnp.concatenate([kv[h][0, link[s][j]] for j in range(NBR)], 0) for s in group]
            vals = [jnp.concatenate([kv[h][1, link[s][j]] for j in range(NBR)], 0) for s in group]
            scores = [dot_nt(qs[s], keys[s]) for s in group]
            grad_w = [dot_nt(gs[s], vals[s]) for s in group]
            low, grad_s = [], []
            for s in group:
                largest = jnp.max(scores[s], axis=-1, keepdims=True)
                expo = jnp.exp2((scores[s] - largest) * (scaling * math.log2(math.e)))
                weights = expo * (1.0 / jnp.sum(expo, axis=-1, keepdims=True))
                low.append(weights.astype(BF16))
                total = jnp.sum(grad_w[s] * weights, axis=-1, keepdims=True)
                grad_s.append((weights * (grad_w[s] - total) * scaling).astype(BF16))
            for s in group:
                store_back(ctx[h], roll_c, s, v, dot_nn(low[s], vals[s]) * keep)
                store_back(dq[h], roll_d, s, v, dot_nn(grad_s[s], keys[s]))
            grad_k = [dot_tn(grad_s[s], qs[s]) for s in group]
            grad_v = [dot_tn(low[s], gs[s]) for s in group]
            for s in group:
                for j in range(NBR):
                    before = before_s[s, j, v]
                    cut = slice(j * HEAD, (j + 1) * HEAD)
                    sum_k[slot[s] + j + 1] = sum_k[before] + grad_k[s][cut]
                    sum_v[slot[s] + j + 1] = sum_v[before] + grad_v[s][cut]
            for when, event in events:
                pl.when(v == min(when, spans - 1))(event)
            return carry

        lax.fori_loop(0, spans, step, 0)

        def gather(b, carry):
            last = last_s[b // HEAD, b % HEAD]
            part[h][0, b] = sum_k[last].astype(BF16)
            part[h][1, b] = sum_v[last].astype(BF16)
            return carry

        lax.fori_loop(0, nz * PLANE, gather, 0)

    send_kv(0)
    send_links()
    wait_kv(0)
    for turn in range(2):
        ag_start(0, 1, turn)
    send_kv(1)
    send_qg(0)
    chain_links()
    forwards = [(step, turn) for step in range(2, far + 1) for turn in range(2)]
    for i, (step, turn) in enumerate(forwards):
        ag_forward(0, step, turn)
        if i == 1:
            send_qg(1)
    wait_kv(1)
    for turn in range(2):
        ag_start(1, 1, turn)
    ag_last(0)
    wait_qg(0)
    at = (AT_A0, AT_A1)
    compute(0, [(at[i], functools.partial(ag_forward, 1, *forwards[i])) for i in range(min(2, len(forwards)))])
    for i, (step, turn) in enumerate(forwards[2:]):
        ag_forward(1, step, turn)
        if i == 1:
            send_out(0)
    rs_begin(0)
    ag_last(1)
    wait_qg(1)
    sums = [(step, turn) for step in range(2, far + 1) for turn in range(2)]
    at = (AT_B0, AT_B1, AT_B2)
    compute(1, [(at[i], functools.partial(rs_step, 0, *sums[i])) for i in range(min(3, len(sums)))])
    rs_begin(1)
    for step, turn in sums[3:]:
        rs_step(0, step, turn)
    send_out(1)
    rs_last(0)
    for step, turn in sums:
        rs_step(1, step, turn)
    rs_last(1)

    wait_bytes(links.at[pl.ds(0, nx - 1)], link_send)
    wait_in_sends()
    for h in range(2):
        for way in range(2):
            for step in range(1, far + 1):
                for kind in range(2):
                    if ag_has(way, step, kind):
                        ag_copy(h, way, step, kind).wait_send()
                    if rs_has(way, step, kind):
                        wait_bytes(rs_dst(h, way, step, kind), rs_send.at[h, way, step - 1, kind])
        wait_bytes(dkv_out.at[:, 0, :, pl.ds(0, (np_ - 1) * HEAD)], out_send.at[h])
        for k, dst in enumerate((ctx_out, dq_out)):
            wait_bytes(dst.at[0, :, pl.ds(0, (np_ - 1) * HEAD)], out_send.at[2 + 2 * k + h])
    for k, dst in enumerate((dkv_out, ctx_out, dq_out)):
        wait_bytes(dst, out_recv.at[k])


def plane_links(neighbours, nz):
    z = lax.axis_index("seq") // PLANE
    per_plane = neighbours.shape[1] // nz
    links = jnp.pad(neighbours[0].T, ((0, 8 - NBR), (1, 0)))
    links = lax.dynamic_slice_in_dim(links, z * per_plane, per_plane + 1, 1)
    return jnp.pad(links, ((0, 0), (0, HEAD - per_plane - 1)))


def solution(mesh):
    nz = mesh.shape["seq"] // PLANE
    nx = mesh.shape["grp"]
    far = nz // 2

    def step(queries, keys_values, neighbours, grad_context):
        links = plane_links(neighbours, nz)
        tokens = queries.shape[1]
        nblk = nz * PLANE
        long_in = 16 + PLANE * tokens + SPAN
        long_out = PLANE * tokens + SPAN
        slots = (PLANE * tokens // SPAN + 1) * nx * NBR
        sem = pltpu.SemaphoreType.DMA
        twice = lambda shape: [pltpu.VMEM(shape, BF16)] * 2
        scratch = (
            twice((2, nblk, HEAD, HEAD))
            + twice((nx, long_in, HEAD)) + twice((nx, long_in, HEAD))
            + twice((nx, long_out, HEAD)) + twice((nx, long_out, HEAD))
            + [pltpu.VMEM((slots + 1, HEAD, HEAD), F32)] * 2
            + twice((2, nblk, HEAD, HEAD))
            + twice((2, PLANE, HEAD, HEAD))
            + twice((2, max(far - 1, 1), 2, PLANE, HEAD, HEAD))
            + twice((2, PLANE, HEAD, HEAD))
            + [pltpu.VMEM((nx, SPAN, HEAD), F32)] * 2
            + [pltpu.VMEM((nx, 8, HEAD), jnp.int32)] * 2 + [pltpu.VMEM((8, HEAD), jnp.int32)]
            + [pltpu.SMEM((nx, 8, HEAD), jnp.int32)] * 2 + [pltpu.SMEM((8, HEAD), jnp.int32)]
            + [sem, sem((3,)), sem((6,)), sem((6,))] + [sem((2, 2, far, 2))] * 4
            + [sem((6,)), sem((3,))]
        )
        hbm = pl.BlockSpec(memory_space=pl.ANY)
        out = pl.pallas_call(
            functools.partial(kernel, nz, nx),
            out_shape=(
                jax.ShapeDtypeStruct(queries.shape, BF16),
                jax.ShapeDtypeStruct(queries.shape, BF16),
                jax.ShapeDtypeStruct(keys_values.shape, BF16),
            ),
            in_specs=[hbm, hbm, hbm, hbm],
            out_specs=(hbm, hbm, hbm),
            scratch_shapes=scratch,
            compiler_params=pltpu.CompilerParams(
                collective_id=0, has_side_effects=True, vmem_limit_bytes=60 * 1024 * 1024
            ),
            name="plane_attention",
        )(links, queries, keys_values, grad_context)
        return tuple(out)

    in_specs = (
        P("grp", "seq", None),
        P(None, "seq", "grp", None),
        P("grp", None, None),
        P("grp", "seq", None),
    )
    out_specs = (P("grp", "seq", None), P("grp", "seq", None), P(None, "seq", "grp", None))
    return jax.shard_map(step, mesh=mesh, in_specs=in_specs, out_specs=out_specs, check_vma=False)
```

```python
import functools
import math

import jax
import jax.numpy as jnp
from jax import lax
from jax.experimental import pallas as pl
from jax.experimental.pallas import tpu as pltpu
from jax.sharding import PartitionSpec as P

SPAN = 64
NBR = 2
HEAD = 128
AT_A = (5, 11)
AT_B = (2, 5, 10, 15)
PLANE = 8
MESH = pl.DeviceIdType.MESH
BF16 = jnp.bfloat16
F32 = jnp.float32


def dot_nt(a, b):
    return lax.dot_general(a, b, (((1,), (1,)), ((), ())), preferred_element_type=F32)


def dot_nn(a, b):
    return lax.dot_general(a, b, (((1,), (0,)), ((), ())), preferred_element_type=F32)


def dot_tn(a, b):
    return lax.dot_general(a, b, (((0,), (0,)), ((), ())), preferred_element_type=F32)


def kernel(nz, nx, links_in, q_in, kv_in, g_in, ctx_out, dq_out, dkv_out,
           kv_a, kv_b, q_a, q_b, g_a, g_b, ctx_a, ctx_b, dq_a, dq_b,
           sum_k, sum_v, part_a, part_b, half_a, half_b, full_a, full_b,
           own_a, own_b, roll_c, roll_d, links, before_v, last_v, links_s, before_s, last_s,
           link_send, link_recv, in_send, in_recv, ag_send, ag_recv, rs_send, rs_recv, out_send, out_recv):
    np_ = nx * PLANE
    tokens = q_in.shape[1]
    rows = kv_in.shape[2]
    spans = PLANE * tokens // SPAN + 1
    far = nz // 2
    scaling = 1.0 / math.sqrt(HEAD)
    seq = lax.axis_index("seq")
    x = lax.axis_index("grp")
    z = seq // PLANE
    yc = seq % PLANE
    me = x * PLANE + yc
    kv = (kv_a, kv_b)
    q = (q_a, q_b)
    g = (g_a, g_b)
    ctx = (ctx_a, ctx_b)
    dq = (dq_a, dq_b)
    part = (part_a, part_b)
    half = (half_a, half_b)
    full = (full_a, full_b)
    own = (own_a, own_b)

    def zone(zz):
        return pl.ds(pl.multiple_of(zz * PLANE, PLANE), PLANE)

    def near(offset):
        return (z + offset + nz) % nz

    def z_device(offset):
        return (near(offset) * PLANE + yc, x)

    def peer(r):
        m = (me + r) % np_
        return m, m // PLANE, m % PLANE

    def columns(m, h):
        return pl.ds(pl.multiple_of((m * 2 + h) * HEAD, HEAD), HEAD)

    zero_rows = jnp.zeros((nx, SPAN, HEAD), BF16)
    for h in range(2):
        for buf in (q[h], g[h]):
            buf[:, :16, :] = jnp.zeros((nx, 16, HEAD), BF16)
            buf[:, 16 + PLANE * tokens:, :] = zero_rows
    sum_k[0] = jnp.zeros((HEAD, HEAD), F32)
    sum_v[0] = jnp.zeros((HEAD, HEAD), F32)

    barrier = pltpu.get_barrier_semaphore()

    def greet(r, carry):
        m, px, pyc = peer(r)
        pl.semaphore_signal(barrier, inc=1, device_id=(z * PLANE + pyc, px), device_id_type=MESH)
        return carry

    lax.fori_loop(1, np_, greet, 0)
    for offset in (-1, 1):
        pl.semaphore_signal(barrier, inc=1, device_id=z_device(offset), device_id_type=MESH)
    pl.semaphore_wait(barrier, np_ + 1)

    def tok_rows(k):
        return pl.ds(pl.multiple_of(16 + k * tokens, 16), tokens)

    def blk_rows(k):
        return pl.ds(pl.multiple_of(k * rows, rows), rows)

    def kv_dst(h, kinds):
        return kv[h].at[kinds, seq, blk_rows(x), :]

    def q_dst(buf):
        return buf.at[x, tok_rows(yc), :]

    def send_kv(h, kinds, sem):
        def body(r, carry):
            m, px, pyc = peer(r)
            pltpu.make_async_remote_copy(
                src_ref=kv_in.at[kinds, 0, :, columns(m, h)], dst_ref=kv_dst(h, kinds),
                send_sem=in_send.at[h], recv_sem=in_recv.at[sem],
                device_id=(z * PLANE + pyc, px), device_id_type=MESH).start()
            return carry
        pltpu.make_async_copy(
            kv_in.at[kinds, 0, :, columns(me, h)], kv_dst(h, kinds), in_recv.at[sem]).start()
        lax.fori_loop(1, np_, body, 0)

    def send_qg(h):
        def body(r, carry):
            m, px, pyc = peer(r)
            for k, (src, dst) in enumerate(((q_in, q[h]), (g_in, g[h]))):
                sem = 2 + 2 * k + h
                pltpu.make_async_remote_copy(
                    src_ref=src.at[0, :, columns(m, h)], dst_ref=q_dst(dst),
                    send_sem=in_send.at[sem], recv_sem=in_recv.at[sem],
                    device_id=(z * PLANE + pyc, px), device_id_type=MESH).start()
            return carry
        for k, (src, dst) in enumerate(((q_in, q[h]), (g_in, g[h]))):
            pltpu.make_async_copy(
                src.at[0, :, columns(me, h)], q_dst(dst), in_recv.at[2 + 2 * k + h]).start()
        lax.fori_loop(1, np_, body, 0)

    def wait_bytes(ref, sem):
        pltpu.make_async_copy(ref, ref, sem).wait()

    def wait_kv(h, kinds, sem):
        wait_bytes(kv[h].at[kinds, zone(z)], in_recv.at[sem])

    def wait_qg(h):
        for k, buf in enumerate((q[h], g[h])):
            wait_bytes(buf.at[:, pl.ds(16, PLANE * tokens), :], in_recv.at[2 + 2 * k + h])

    def wait_in_sends():
        for h in range(2):
            wait_bytes(kv_in.at[:, 0, :, pl.ds(0, (np_ - 1) * HEAD)], in_send.at[h])
            for k, src in enumerate((q_in, g_in)):
                wait_bytes(src.at[0, :, pl.ds(0, (np_ - 1) * HEAD)], in_send.at[2 + 2 * k + h])

    def send_links():
        def body(r, carry):
            pltpu.make_async_remote_copy(
                src_ref=links_in, dst_ref=links.at[x], send_sem=link_send, recv_sem=link_recv.at[0],
                device_id=(seq, (x + r) % nx), device_id_type=MESH).start()
            return carry
        pltpu.make_async_copy(links_in, links.at[x], link_recv.at[0]).start()
        lax.fori_loop(1, nx, body, 0)

    def chain_links():
        wait_bytes(links, link_recv.at[0])
        copy = pltpu.make_async_copy(links, links_s, link_recv.at[1])
        copy.start()
        copy.wait()
        shape = links.shape[1:]
        row = lax.broadcasted_iota(jnp.int32, shape, 0)
        lane = lax.broadcasted_iota(jnp.int32, shape, 1)
        block = row * shape[1] + lane
        held = [links[s] for s in range(nx)]
        slot = [(lane * nx + s) * NBR + row + 1 for s in range(nx)]

        def body(v, carry):
            before, last = list(carry[:nx]), carry[nx]
            for s in range(nx):
                for j in range(NBR):
                    link = links_s[s, j, v]
                    here = (v * nx + s) * NBR + j + 1
                    for t in range(nx):
                        before[t] = jnp.where(
                            jnp.logical_and(held[t] == link, slot[t] > here), here, before[t])
                    last = jnp.where(block == link, here, last)
            return (*before, last)

        zero = jnp.zeros(shape, jnp.int32)
        found = lax.fori_loop(0, spans, body, (zero,) * (nx + 1))
        for s in range(nx):
            before_v[s] = found[s]
        last_v[...] = found[nx]
        copies = (pltpu.make_async_copy(before_v, before_s, link_recv.at[1]),
                  pltpu.make_async_copy(last_v, last_s, link_recv.at[2]))
        for copy in copies:
            copy.start()
        for copy in copies:
            copy.wait()

    def zone_part(zz, way, split):
        if split:
            return pl.ds(zz * PLANE + way * (PLANE // 2), PLANE // 2)
        return zone(zz)

    def ag_ref(h, way, step, kind, hops):
        return kv[h].at[kind, zone_part(near((2 * way - 1) * hops), way, step == far)]

    def ag_copy(h, way, step, kind):
        ref = ag_ref(h, way, step, kind, step - 1)
        return pltpu.make_async_remote_copy(
            src_ref=ref, dst_ref=ref,
            send_sem=ag_send.at[h, way, step - 1, kind], recv_sem=ag_recv.at[h, way, step - 1, kind],
            device_id=z_device(1 - 2 * way), device_id_type=MESH)

    def ag_start(h, kind):
        for way in range(2):
            ag_copy(h, way, 1, kind).start()

    def ag_wait(h, way, step, kind):
        wait_bytes(ag_ref(h, way, step, kind, step), ag_recv.at[h, way, step - 1, kind])

    def ag_forward(h, step, kind):
        for way in range(2):
            ag_wait(h, way, step - 1, kind)
            ag_copy(h, way, step, kind).start()

    def ag_last(h):
        for kind in range(2):
            for way in range(2):
                ag_wait(h, way, far, kind)

    def rs_dst(h, way, step, kind):
        return half[h].at[way, kind] if step == 1 else full[h].at[way, step - 2, kind]

    def rs_send_part(h, way, step, kind):
        zz = near((1 - 2 * way) * (far + 1 - step))
        pltpu.make_async_remote_copy(
            src_ref=part[h].at[kind, zone_part(zz, way, step == 1)], dst_ref=rs_dst(h, way, step, kind),
            send_sem=rs_send.at[h, way, step - 1, kind], recv_sem=rs_recv.at[h, way, step - 1, kind],
            device_id=z_device(1 - 2 * way), device_id_type=MESH).start()

    def rs_wait(h, way, step, kind):
        wait_bytes(rs_dst(h, way, step, kind), rs_recv.at[h, way, step - 1, kind])

    def rs_begin(h):
        for kind in range(2):
            for way in range(2):
                rs_send_part(h, way, 1, kind)

    def rs_step(h, step, kind):
        for way in range(2):
            rs_wait(h, way, step - 1, kind)
            got = rs_dst(h, way, step - 1, kind)
            base = near((1 - 2 * way) * (far + 1 - step)) * PLANE
            if step == 2:
                base = base + way * (PLANE // 2)

            def add(b, carry):
                part[h][kind, base + b] = (
                    part[h][kind, base + b].astype(F32) + got[b].astype(F32)).astype(BF16)
                return carry

            lax.fori_loop(0, PLANE // 2 if step == 2 else PLANE, add, 0)
            rs_send_part(h, way, step, kind)

    def rs_last(h, kind):
        for way in range(2):
            rs_wait(h, way, far, kind)

        def add(b, carry):
            total = part[h][kind, z * PLANE + b].astype(F32)
            for way in range(2):
                total += rs_dst(h, way, far, kind)[b].astype(F32)
            own[h][kind, b] = total.astype(BF16)
            return carry

        lax.fori_loop(0, PLANE, add, 0)

    def send_own(h, kinds):
        def body(r, carry):
            m, px, pyc = peer(r)
            pltpu.make_async_remote_copy(
                src_ref=own[h].at[kinds, pyc, blk_rows(px), :], dst_ref=dkv_out.at[kinds, 0, :, columns(me, h)],
                send_sem=out_send.at[h], recv_sem=out_recv.at[0],
                device_id=(z * PLANE + pyc, px), device_id_type=MESH).start()
            return carry

        pltpu.make_async_copy(
            own[h].at[kinds, yc, blk_rows(x), :], dkv_out.at[kinds, 0, :, columns(me, h)],
            out_recv.at[0]).start()
        lax.fori_loop(1, np_, body, 0)

    def out_rows(k):
        return pl.ds(pl.multiple_of(SPAN + k * tokens, 16), tokens)

    def send_out(h):
        def body(r, carry):
            m, px, pyc = peer(r)
            for k, (src, dst) in enumerate(((ctx[h], ctx_out), (dq[h], dq_out))):
                pltpu.make_async_remote_copy(
                    src_ref=src.at[px, out_rows(pyc), :], dst_ref=dst.at[0, :, columns(me, h)],
                    send_sem=out_send.at[2 + 2 * k + h], recv_sem=out_recv.at[1 + k],
                    device_id=(z * PLANE + pyc, px), device_id_type=MESH).start()
            return carry
        for k, (src, dst) in enumerate(((ctx[h], ctx_out), (dq[h], dq_out))):
            pltpu.make_async_copy(
                src.at[x, out_rows(yc), :], dst.at[0, :, columns(me, h)], out_recv.at[1 + k]).start()
        lax.fori_loop(1, np_, body, 0)

    def compute(h, events):
        row_id = lax.broadcasted_iota(jnp.int32, (SPAN, HEAD), 0)

        def shifted(buf, s, v):
            wide = buf[s, pl.ds(pl.multiple_of(v * SPAN, SPAN), SPAN + 16), :].astype(F32)
            return pltpu.roll(wide, SPAN + 1, 0)[:SPAN]

        def store_back(out, hold, s, v, value):
            rolled = pltpu.roll(value, SPAN - 1, 0)
            out[s, pl.ds(pl.multiple_of(v * SPAN, SPAN), SPAN), :] = jnp.where(
                row_id == SPAN - 1, rolled, hold[s]).astype(BF16)
            hold[s] = rolled

        def step(v, carry):
            head_start = jnp.logical_and(z == 0, v == 0)
            keep = jnp.where(head_start, 0.0, 1.0)
            group = range(nx)
            slot = [(v * nx + s) * NBR for s in group]
            link = [[links_s[s, j, v] for j in range(NBR)] for s in group]
            qs = [shifted(q[h], s, v).astype(BF16) for s in group]
            gs = [(shifted(g[h], s, v) * keep).astype(BF16) for s in group]
            keys = [jnp.concatenate([kv[h][0, link[s][j]] for j in range(NBR)], 0) for s in group]
            vals = [jnp.concatenate([kv[h][1, link[s][j]] for j in range(NBR)], 0) for s in group]
            scores = [dot_nt(qs[s], keys[s]) for s in group]
            grad_w = [dot_nt(gs[s], vals[s]) for s in group]
            low, grad_s = [], []
            for s in group:
                largest = jnp.max(scores[s], axis=-1, keepdims=True)
                expo = jnp.exp2((scores[s] - largest) * (scaling * math.log2(math.e)))
                weights = expo * (1.0 / jnp.sum(expo, axis=-1, keepdims=True))
                low.append(weights.astype(BF16))
                total = jnp.sum(grad_w[s] * weights, axis=-1, keepdims=True)
                grad_s.append((weights * (grad_w[s] - total) * scaling).astype(BF16))
            for s in group:
                store_back(ctx[h], roll_c, s, v, dot_nn(low[s], vals[s]) * keep)
                store_back(dq[h], roll_d, s, v, dot_nn(grad_s[s], keys[s]))
            grad_k = [dot_tn(grad_s[s], qs[s]) for s in group]
            grad_v = [dot_tn(low[s], gs[s]) for s in group]
            for s in group:
                for j in range(NBR):
                    before = before_s[s, j, v]
                    cut = slice(j * HEAD, (j + 1) * HEAD)
                    sum_k[slot[s] + j + 1] = sum_k[before] + grad_k[s][cut]
                    sum_v[slot[s] + j + 1] = sum_v[before] + grad_v[s][cut]
            for when, event in events:
                pl.when(v == min(when, spans - 1))(event)
            return carry

        lax.fori_loop(0, spans, step, 0)

        def gather(b, carry):
            last = last_s[b // HEAD, b % HEAD]
            part[h][0, b] = sum_k[last].astype(BF16)
            part[h][1, b] = sum_v[last].astype(BF16)
            return carry

        lax.fori_loop(0, nz * PLANE, gather, 0)

    both = pl.ds(0, 2)
    for kind in range(2):
        send_kv(0, pl.ds(kind, 1), 6 * kind)
    send_links()
    for kind in range(2):
        wait_kv(0, pl.ds(kind, 1), 6 * kind)
        ag_start(0, kind)
    send_kv(1, both, 1)
    send_qg(0)
    chain_links()
    steps = [(step, kind) for step in range(2, far + 1) for kind in range(2)]
    for i, (step, kind) in enumerate(steps):
        ag_forward(0, step, kind)
        if i == 1:
            send_qg(1)
    wait_kv(1, both, 1)
    for kind in range(2):
        ag_start(1, kind)
    ag_last(0)
    wait_qg(0)
    compute(0, [(when, functools.partial(ag_forward, 1, *todo)) for when, todo in zip(AT_A, steps)])
    for i, (step, kind) in enumerate(steps[len(AT_A):]):
        ag_forward(1, step, kind)
        if i == 1:
            send_out(0)
    rs_begin(0)
    ag_last(1)
    wait_qg(1)
    compute(1, [(when, functools.partial(rs_step, 0, *todo)) for when, todo in zip(AT_B, steps)])
    rs_begin(1)
    for i, (step, kind) in enumerate(steps[len(AT_B):]):
        rs_step(0, step, kind)
        if i == 1:
            send_out(1)
    for kind in range(2):
        rs_last(0, kind)
    send_own(0, both)
    for step, kind in steps:
        rs_step(1, step, kind)
    for kind in range(2):
        rs_last(1, kind)
        send_own(1, pl.ds(kind, 1))

    wait_bytes(links.at[pl.ds(0, nx - 1)], link_send)
    wait_in_sends()
    for h in range(2):
        for way in range(2):
            for step in range(1, far + 1):
                for kind in range(2):
                    ag_copy(h, way, step, kind).wait_send()
                    wait_bytes(rs_dst(h, way, step, kind), rs_send.at[h, way, step - 1, kind])
        wait_bytes(dkv_out.at[:, 0, :, pl.ds(0, (np_ - 1) * HEAD)], out_send.at[h])
        for k, dst in enumerate((ctx_out, dq_out)):
            wait_bytes(dst.at[0, :, pl.ds(0, (np_ - 1) * HEAD)], out_send.at[2 + 2 * k + h])
    for k, dst in enumerate((dkv_out, ctx_out, dq_out)):
        wait_bytes(dst, out_recv.at[k])


def finish(a, b, c):
    def body(*refs):
        sems = refs[6]
        copies = []
        for k in range(3):
            rows = refs[k].shape[-2] // 2
            lead = (slice(None),) * (len(refs[k].shape) - 2)
            for part in range(2):
                at = lead + (pl.ds(part * rows, rows),)
                copies.append(pltpu.make_async_copy(
                    refs[k].at[at], refs[3 + k].at[at], sems.at[2 * k + part]))
        for copy in copies:
            copy.start()
        for copy in copies:
            copy.wait()

    hbm = pl.BlockSpec(memory_space=pl.ANY)
    return pl.pallas_call(
        body,
        out_shape=tuple(jax.ShapeDtypeStruct(t.shape, t.dtype) for t in (a, b, c)),
        in_specs=[hbm] * 3, out_specs=(hbm,) * 3,
        scratch_shapes=[pltpu.SemaphoreType.DMA((6,))],
        name="results",
    )(a, b, c)


def plane_links(neighbours, nz):
    z = lax.axis_index("seq") // PLANE
    per_plane = neighbours.shape[1] // nz
    links = jnp.pad(neighbours[0].T, ((0, 8 - NBR), (1, 0)))
    links = lax.dynamic_slice_in_dim(links, z * per_plane, per_plane + 1, 1)
    return jnp.pad(links, ((0, 0), (0, HEAD - per_plane - 1)))


def solution(mesh):
    nz = mesh.shape["seq"] // PLANE
    nx = mesh.shape["grp"]
    far = nz // 2

    def step(queries, keys_values, neighbours, grad_context):
        links = plane_links(neighbours, nz)
        tokens = queries.shape[1]
        nblk = nz * PLANE
        long_in = 16 + PLANE * tokens + SPAN
        long_out = PLANE * tokens + SPAN
        slots = (PLANE * tokens // SPAN + 1) * nx * NBR
        sem = pltpu.SemaphoreType.DMA
        twice = lambda shape: [pltpu.VMEM(shape, BF16)] * 2
        scratch = (
            twice((2, nblk, HEAD, HEAD))
            + twice((nx, long_in, HEAD)) + twice((nx, long_in, HEAD))
            + twice((nx, long_out, HEAD)) + twice((nx, long_out, HEAD))
            + [pltpu.VMEM((slots + 1, HEAD, HEAD), F32)] * 2
            + twice((2, nblk, HEAD, HEAD))
            + twice((2, 2, PLANE // 2, HEAD, HEAD))
            + twice((2, max(far - 1, 1), 2, PLANE, HEAD, HEAD))
            + twice((2, PLANE, HEAD, HEAD))
            + [pltpu.VMEM((nx, SPAN, HEAD), F32)] * 2
            + [pltpu.VMEM((nx, 8, HEAD), jnp.int32)] * 2 + [pltpu.VMEM((8, HEAD), jnp.int32)]
            + [pltpu.SMEM((nx, 8, HEAD), jnp.int32)] * 2 + [pltpu.SMEM((8, HEAD), jnp.int32)]
            + [sem, sem((3,)), sem((6,)), sem((7,))] + [sem((2, 2, far, 2))] * 4
            + [sem((6,)), sem((3,))]
        )
        hbm = pl.BlockSpec(memory_space=pl.ANY)
        out = pl.pallas_call(
            functools.partial(kernel, nz, nx),
            out_shape=(
                jax.ShapeDtypeStruct(queries.shape, BF16),
                jax.ShapeDtypeStruct(queries.shape, BF16),
                jax.ShapeDtypeStruct(keys_values.shape, BF16),
            ),
            in_specs=[hbm, hbm, hbm, hbm],
            out_specs=(hbm, hbm, hbm),
            scratch_shapes=scratch,
            compiler_params=pltpu.CompilerParams(
                collective_id=0, has_side_effects=True, vmem_limit_bytes=60 * 1024 * 1024
            ),
            name="plane_attention",
        )(links, queries, keys_values, grad_context)
        return tuple(out)

    in_specs = (
        P("grp", "seq", None),
        P(None, "seq", "grp", None),
        P("grp", None, None),
        P("grp", "seq", None),
    )
    out_specs = (P("grp", "seq", None), P("grp", "seq", None), P(None, "seq", "grp", None))
    return jax.shard_map(step, mesh=mesh, in_specs=in_specs, out_specs=out_specs, check_vma=False)
```

```python
import functools
import math

import jax
import jax.numpy as jnp
from jax import lax
from jax.experimental import pallas as pl
from jax.experimental.pallas import tpu as pltpu
from jax.sharding import PartitionSpec as P

SPAN = 64
NBR = 2
HEAD = 128
AT_A = (5, 11)
AT_B = (2, 5, 10, 15)
PLANE = 8
MESH = pl.DeviceIdType.MESH
BF16 = jnp.bfloat16
F32 = jnp.float32


def dot_nt(a, b):
    return lax.dot_general(a, b, (((1,), (1,)), ((), ())), preferred_element_type=F32)


def dot_nn(a, b):
    return lax.dot_general(a, b, (((1,), (0,)), ((), ())), preferred_element_type=F32)


def dot_tn(a, b):
    return lax.dot_general(a, b, (((0,), (0,)), ((), ())), preferred_element_type=F32)


def kernel(nz, nx, links_in, q_in, kv_in, g_in, ctx_out, dq_out, dkv_out,
           kv_a, kv_b, q_a, q_b, g_a, g_b, ctx_a, ctx_b, dq_a, dq_b,
           sum_k, sum_v, part_a, part_b, half_a, half_b, full_a, full_b,
           own_a, own_b, roll_c, roll_d, links, before_v, last_v, links_s, before_s, last_s,
           link_send, link_recv, in_send, in_recv, ag_send, ag_recv, rs_send, rs_recv, out_send, out_recv):
    np_ = nx * PLANE
    tokens = q_in.shape[1]
    rows = kv_in.shape[2]
    spans = PLANE * tokens // SPAN + 1
    far = nz // 2
    scaling = 1.0 / math.sqrt(HEAD)
    seq = lax.axis_index("seq")
    x = lax.axis_index("grp")
    z = seq // PLANE
    yc = seq % PLANE
    me = x * PLANE + yc
    kv = (kv_a, kv_b)
    q = (q_a, q_b)
    g = (g_a, g_b)
    ctx = (ctx_a, ctx_b)
    dq = (dq_a, dq_b)
    part = (part_a, part_b)
    half = (half_a, half_b)
    full = (full_a, full_b)
    own = (own_a, own_b)

    def zone(zz):
        return pl.ds(pl.multiple_of(zz * PLANE, PLANE), PLANE)

    def near(offset):
        return (z + offset + nz) % nz

    def z_device(offset):
        return (near(offset) * PLANE + yc, x)

    def peer(r):
        m = (me + r) % np_
        return m, m // PLANE, m % PLANE

    def columns(m, h):
        return pl.ds(pl.multiple_of((m * 2 + h) * HEAD, HEAD), HEAD)

    zero_rows = jnp.zeros((nx, SPAN, HEAD), BF16)
    for h in range(2):
        for buf in (q[h], g[h]):
            buf[:, :16, :] = jnp.zeros((nx, 16, HEAD), BF16)
            buf[:, 16 + PLANE * tokens:, :] = zero_rows
    sum_k[0] = jnp.zeros((HEAD, HEAD), F32)
    sum_v[0] = jnp.zeros((HEAD, HEAD), F32)

    barrier = pltpu.get_barrier_semaphore()

    def greet(r, carry):
        m, px, pyc = peer(r)
        pl.semaphore_signal(barrier, inc=1, device_id=(z * PLANE + pyc, px), device_id_type=MESH)
        return carry

    lax.fori_loop(1, np_, greet, 0)
    for offset in (-1, 1):
        pl.semaphore_signal(barrier, inc=1, device_id=z_device(offset), device_id_type=MESH)
    pl.semaphore_wait(barrier, np_ + 1)

    def tok_rows(k):
        return pl.ds(pl.multiple_of(16 + k * tokens, 16), tokens)

    def blk_rows(k):
        return pl.ds(pl.multiple_of(k * rows, rows), rows)

    def kv_dst(h, kinds):
        return kv[h].at[kinds, seq, blk_rows(x), :]

    def q_dst(buf):
        return buf.at[x, tok_rows(yc), :]

    def send_kv(h, kinds, sem):
        def body(r, carry):
            m, px, pyc = peer(r)
            pltpu.make_async_remote_copy(
                src_ref=kv_in.at[kinds, 0, :, columns(m, h)], dst_ref=kv_dst(h, kinds),
                send_sem=in_send.at[h], recv_sem=in_recv.at[sem],
                device_id=(z * PLANE + pyc, px), device_id_type=MESH).start()
            return carry
        pltpu.make_async_copy(
            kv_in.at[kinds, 0, :, columns(me, h)], kv_dst(h, kinds), in_recv.at[sem]).start()
        lax.fori_loop(1, np_, body, 0)

    def send_qg(h):
        def body(r, carry):
            m, px, pyc = peer(r)
            for k, (src, dst) in enumerate(((q_in, q[h]), (g_in, g[h]))):
                sem = 2 + 2 * k + h
                pltpu.make_async_remote_copy(
                    src_ref=src.at[0, :, columns(m, h)], dst_ref=q_dst(dst),
                    send_sem=in_send.at[sem], recv_sem=in_recv.at[sem],
                    device_id=(z * PLANE + pyc, px), device_id_type=MESH).start()
            return carry
        for k, (src, dst) in enumerate(((q_in, q[h]), (g_in, g[h]))):
            pltpu.make_async_copy(
                src.at[0, :, columns(me, h)], q_dst(dst), in_recv.at[2 + 2 * k + h]).start()
        lax.fori_loop(1, np_, body, 0)

    def wait_bytes(ref, sem):
        pltpu.make_async_copy(ref, ref, sem).wait()

    def wait_kv(h, kinds, sem):
        wait_bytes(kv[h].at[kinds, zone(z)], in_recv.at[sem])

    def wait_qg(h):
        for k, buf in enumerate((q[h], g[h])):
            wait_bytes(buf.at[:, pl.ds(16, PLANE * tokens), :], in_recv.at[2 + 2 * k + h])

    def wait_in_sends():
        for h in range(2):
            wait_bytes(kv_in.at[:, 0, :, pl.ds(0, (np_ - 1) * HEAD)], in_send.at[h])
            for k, src in enumerate((q_in, g_in)):
                wait_bytes(src.at[0, :, pl.ds(0, (np_ - 1) * HEAD)], in_send.at[2 + 2 * k + h])

    def send_links():
        def body(r, carry):
            pltpu.make_async_remote_copy(
                src_ref=links_in, dst_ref=links.at[x], send_sem=link_send, recv_sem=link_recv.at[0],
                device_id=(seq, (x + r) % nx), device_id_type=MESH).start()
            return carry
        pltpu.make_async_copy(links_in, links.at[x], link_recv.at[0]).start()
        lax.fori_loop(1, nx, body, 0)

    def chain_links():
        wait_bytes(links, link_recv.at[0])
        copy = pltpu.make_async_copy(links, links_s, link_recv.at[1])
        copy.start()
        copy.wait()
        shape = links.shape[1:]
        row = lax.broadcasted_iota(jnp.int32, shape, 0)
        lane = lax.broadcasted_iota(jnp.int32, shape, 1)
        block = row * shape[1] + lane
        held = [links[s] for s in range(nx)]
        slot = [(lane * nx + s) * NBR + row + 1 for s in range(nx)]

        def body(v, carry):
            before, last = list(carry[:nx]), carry[nx]
            for s in range(nx):
                for j in range(NBR):
                    link = links_s[s, j, v]
                    here = (v * nx + s) * NBR + j + 1
                    for t in range(nx):
                        before[t] = jnp.where(
                            jnp.logical_and(held[t] == link, slot[t] > here), here, before[t])
                    last = jnp.where(block == link, here, last)
            return (*before, last)

        zero = jnp.zeros(shape, jnp.int32)
        found = lax.fori_loop(0, spans, body, (zero,) * (nx + 1))
        for s in range(nx):
            before_v[s] = found[s]
        last_v[...] = found[nx]
        copies = (pltpu.make_async_copy(before_v, before_s, link_recv.at[1]),
                  pltpu.make_async_copy(last_v, last_s, link_recv.at[2]))
        for copy in copies:
            copy.start()
        for copy in copies:
            copy.wait()

    def zone_part(zz, way, split):
        if split:
            return pl.ds(zz * PLANE + way * (PLANE // 2), PLANE // 2)
        return zone(zz)

    def ag_ref(h, way, step, kind, hops):
        return kv[h].at[kind, zone_part(near((2 * way - 1) * hops), way, step == far)]

    def ag_copy(h, way, step, kind):
        ref = ag_ref(h, way, step, kind, step - 1)
        return pltpu.make_async_remote_copy(
            src_ref=ref, dst_ref=ref,
            send_sem=ag_send.at[h, way, step - 1, kind], recv_sem=ag_recv.at[h, way, step - 1, kind],
            device_id=z_device(1 - 2 * way), device_id_type=MESH)

    def ag_start(h, kind):
        for way in range(2):
            ag_copy(h, way, 1, kind).start()

    def ag_wait(h, way, step, kind):
        wait_bytes(ag_ref(h, way, step, kind, step), ag_recv.at[h, way, step - 1, kind])

    def ag_forward(h, step, kind):
        for way in range(2):
            ag_wait(h, way, step - 1, kind)
            ag_copy(h, way, step, kind).start()

    def ag_last(h):
        for kind in range(2):
            for way in range(2):
                ag_wait(h, way, far, kind)

    def rs_dst(h, way, step, kind):
        return half[h].at[way, kind] if step == 1 else full[h].at[way, step - 2, kind]

    def rs_send_part(h, way, step, kind):
        zz = near((1 - 2 * way) * (far + 1 - step))
        pltpu.make_async_remote_copy(
            src_ref=part[h].at[kind, zone_part(zz, way, step == 1)], dst_ref=rs_dst(h, way, step, kind),
            send_sem=rs_send.at[h, way, step - 1, kind], recv_sem=rs_recv.at[h, way, step - 1, kind],
            device_id=z_device(1 - 2 * way), device_id_type=MESH).start()

    def rs_wait(h, way, step, kind):
        wait_bytes(rs_dst(h, way, step, kind), rs_recv.at[h, way, step - 1, kind])

    def rs_begin(h):
        for kind in range(2):
            for way in range(2):
                rs_send_part(h, way, 1, kind)

    def rs_step(h, step, kind):
        for way in range(2):
            rs_wait(h, way, step - 1, kind)
            got = rs_dst(h, way, step - 1, kind)
            base = near((1 - 2 * way) * (far + 1 - step)) * PLANE
            if step == 2:
                base = base + way * (PLANE // 2)

            def add(b, carry):
                part[h][kind, base + b] = (
                    part[h][kind, base + b].astype(F32) + got[b].astype(F32)).astype(BF16)
                return carry

            lax.fori_loop(0, PLANE // 2 if step == 2 else PLANE, add, 0)
            rs_send_part(h, way, step, kind)

    def rs_last(h, kind):
        for way in range(2):
            rs_wait(h, way, far, kind)

        def add(b, carry):
            total = part[h][kind, z * PLANE + b].astype(F32)
            for way in range(2):
                total += rs_dst(h, way, far, kind)[b].astype(F32)
            own[h][kind, b] = total.astype(BF16)
            return carry

        lax.fori_loop(0, PLANE, add, 0)

    def send_own(h, kinds):
        def body(r, carry):
            m, px, pyc = peer(r)
            pltpu.make_async_remote_copy(
                src_ref=own[h].at[kinds, pyc, blk_rows(px), :], dst_ref=dkv_out.at[kinds, 0, :, columns(me, h)],
                send_sem=out_send.at[h], recv_sem=out_recv.at[0],
                device_id=(z * PLANE + pyc, px), device_id_type=MESH).start()
            return carry

        pltpu.make_async_copy(
            own[h].at[kinds, yc, blk_rows(x), :], dkv_out.at[kinds, 0, :, columns(me, h)],
            out_recv.at[0]).start()
        lax.fori_loop(1, np_, body, 0)

    def out_rows(k):
        return pl.ds(pl.multiple_of(SPAN + k * tokens, 16), tokens)

    def send_out(h):
        def body(r, carry):
            m, px, pyc = peer(r)
            for k, (src, dst) in enumerate(((ctx[h], ctx_out), (dq[h], dq_out))):
                pltpu.make_async_remote_copy(
                    src_ref=src.at[px, out_rows(pyc), :], dst_ref=dst.at[0, :, columns(me, h)],
                    send_sem=out_send.at[2 + 2 * k + h], recv_sem=out_recv.at[1 + k],
                    device_id=(z * PLANE + pyc, px), device_id_type=MESH).start()
            return carry
        for k, (src, dst) in enumerate(((ctx[h], ctx_out), (dq[h], dq_out))):
            pltpu.make_async_copy(
                src.at[x, out_rows(yc), :], dst.at[0, :, columns(me, h)], out_recv.at[1 + k]).start()
        lax.fori_loop(1, np_, body, 0)

    def compute(h, events):
        row_id = lax.broadcasted_iota(jnp.int32, (SPAN, HEAD), 0)

        def shifted(buf, s, v):
            wide = buf[s, pl.ds(pl.multiple_of(v * SPAN, SPAN), SPAN + 16), :].astype(F32)
            return pltpu.roll(wide, SPAN + 1, 0)[:SPAN]

        def store_back(out, hold, s, v, value):
            rolled = pltpu.roll(value, SPAN - 1, 0)
            out[s, pl.ds(pl.multiple_of(v * SPAN, SPAN), SPAN), :] = jnp.where(
                row_id == SPAN - 1, rolled, hold[s]).astype(BF16)
            hold[s] = rolled

        def step(v, carry):
            head_start = jnp.logical_and(z == 0, v == 0)
            keep = jnp.where(head_start, 0.0, 1.0)
            group = range(nx)
            slot = [(v * nx + s) * NBR for s in group]
            link = [[links_s[s, j, v] for j in range(NBR)] for s in group]
            qs = [shifted(q[h], s, v).astype(BF16) for s in group]
            gs = [(shifted(g[h], s, v) * keep).astype(BF16) for s in group]
            keys = [jnp.concatenate([kv[h][0, link[s][j]] for j in range(NBR)], 0) for s in group]
            vals = [jnp.concatenate([kv[h][1, link[s][j]] for j in range(NBR)], 0) for s in group]
            scores = [dot_nt(qs[s], keys[s]) for s in group]
            grad_w = [dot_nt(gs[s], vals[s]) for s in group]
            low, grad_s = [], []
            for s in group:
                largest = jnp.max(scores[s], axis=-1, keepdims=True)
                expo = jnp.exp2((scores[s] - largest) * (scaling * math.log2(math.e)))
                weights = expo * (1.0 / jnp.sum(expo, axis=-1, keepdims=True))
                low.append(weights.astype(BF16))
                total = jnp.sum(grad_w[s] * weights, axis=-1, keepdims=True)
                grad_s.append((weights * (grad_w[s] - total) * scaling).astype(BF16))
            for s in group:
                store_back(ctx[h], roll_c, s, v, dot_nn(low[s], vals[s]) * keep)
                store_back(dq[h], roll_d, s, v, dot_nn(grad_s[s], keys[s]))
            grad_k = [dot_tn(grad_s[s], qs[s]) for s in group]
            grad_v = [dot_tn(low[s], gs[s]) for s in group]
            for s in group:
                for j in range(NBR):
                    before = before_s[s, j, v]
                    cut = slice(j * HEAD, (j + 1) * HEAD)
                    sum_k[slot[s] + j + 1] = sum_k[before] + grad_k[s][cut]
                    sum_v[slot[s] + j + 1] = sum_v[before] + grad_v[s][cut]
            for when, event in events:
                pl.when(v == min(when, spans - 1))(event)
            return carry

        lax.fori_loop(0, spans, step, 0)

        def gather(b, carry):
            last = last_s[b // HEAD, b % HEAD]
            part[h][0, b] = sum_k[last].astype(BF16)
            part[h][1, b] = sum_v[last].astype(BF16)
            return carry

        lax.fori_loop(0, nz * PLANE, gather, 0)

    both = pl.ds(0, 2)
    for kind in range(2):
        send_kv(0, pl.ds(kind, 1), 6 * kind)
    send_links()
    for kind in range(2):
        wait_kv(0, pl.ds(kind, 1), 6 * kind)
        ag_start(0, kind)
    send_kv(1, both, 1)
    send_qg(0)
    chain_links()
    steps = [(step, kind) for step in range(2, far + 1) for kind in range(2)]
    for i, (step, kind) in enumerate(steps):
        ag_forward(0, step, kind)
        if i == 1:
            send_qg(1)
    wait_kv(1, both, 1)
    for kind in range(2):
        ag_start(1, kind)
    ag_last(0)
    wait_qg(0)
    compute(0, [(when, functools.partial(ag_forward, 1, *todo)) for when, todo in zip(AT_A, steps)])
    for i, (step, kind) in enumerate(steps[len(AT_A):]):
        ag_forward(1, step, kind)
        if i == 1:
            send_out(0)
    rs_begin(0)
    ag_last(1)
    wait_qg(1)
    compute(1, [(when, functools.partial(rs_step, 0, *todo)) for when, todo in zip(AT_B, steps)])
    rs_begin(1)
    for i, (step, kind) in enumerate(steps[len(AT_B):]):
        rs_step(0, step, kind)
        if i == 1:
            send_out(1)
    for kind in range(2):
        rs_last(0, kind)
    send_own(0, both)
    for step, kind in steps:
        rs_step(1, step, kind)
    for kind in range(2):
        rs_last(1, kind)
        send_own(1, pl.ds(kind, 1))

    wait_bytes(links.at[pl.ds(0, nx - 1)], link_send)
    wait_in_sends()
    for h in range(2):
        for way in range(2):
            for step in range(1, far + 1):
                for kind in range(2):
                    ag_copy(h, way, step, kind).wait_send()
                    wait_bytes(rs_dst(h, way, step, kind), rs_send.at[h, way, step - 1, kind])
        wait_bytes(dkv_out.at[:, 0, :, pl.ds(0, (np_ - 1) * HEAD)], out_send.at[h])
        for k, dst in enumerate((ctx_out, dq_out)):
            wait_bytes(dst.at[0, :, pl.ds(0, (np_ - 1) * HEAD)], out_send.at[2 + 2 * k + h])
    for k, dst in enumerate((dkv_out, ctx_out, dq_out)):
        wait_bytes(dst, out_recv.at[k])


def results(*arrays):
    n = len(arrays)

    def body(*refs):
        src, dst, held, (sem_in, sem_out) = refs[:n], refs[n:2 * n], refs[2 * n:3 * n], refs[3 * n:]
        cuts = []
        for k in range(n):
            rows = src[k].shape[-2]
            for lead in range(src[k].shape[0]):
                for r in range(0, rows, 32):
                    cuts.append((k, (lead,) + (0,) * (len(src[k].shape) - 3) + (pl.ds(r, 32),)))
        loads = [pltpu.make_async_copy(src[k].at[at], held[k].at[at], sem_in.at[i])
                 for i, (k, at) in enumerate(cuts)]
        stores = [pltpu.make_async_copy(held[k].at[at], dst[k].at[at], sem_out.at[i])
                  for i, (k, at) in enumerate(cuts)]
        for copy in loads:
            copy.start()
        for load, store in zip(loads, stores):
            load.wait()
            store.start()
        for copy in stores:
            copy.wait()

    hbm = pl.BlockSpec(memory_space=pl.ANY)
    count = sum(t.shape[0] * (t.shape[-2] // 32) for t in arrays)
    return pl.pallas_call(
        body,
        out_shape=tuple(jax.ShapeDtypeStruct(t.shape, t.dtype) for t in arrays),
        in_specs=[hbm] * n, out_specs=(hbm,) * n,
        scratch_shapes=[pltpu.VMEM(t.shape, t.dtype) for t in arrays]
        + [pltpu.SemaphoreType.DMA((count,))] * 2,
        compiler_params=pltpu.CompilerParams(vmem_limit_bytes=60 * 1024 * 1024),
        name="results",
    )(*arrays)


def plane_links(neighbours, nz):
    z = lax.axis_index("seq") // PLANE
    per_plane = neighbours.shape[1] // nz
    links = jnp.pad(neighbours[0].T, ((0, 8 - NBR), (1, 0)))
    links = lax.dynamic_slice_in_dim(links, z * per_plane, per_plane + 1, 1)
    return jnp.pad(links, ((0, 0), (0, HEAD - per_plane - 1)))


def solution(mesh):
    nz = mesh.shape["seq"] // PLANE
    nx = mesh.shape["grp"]
    far = nz // 2

    def step(queries, keys_values, neighbours, grad_context):
        links = plane_links(neighbours, nz)
        tokens = queries.shape[1]
        nblk = nz * PLANE
        long_in = 16 + PLANE * tokens + SPAN
        long_out = PLANE * tokens + SPAN
        slots = (PLANE * tokens // SPAN + 1) * nx * NBR
        sem = pltpu.SemaphoreType.DMA
        twice = lambda shape: [pltpu.VMEM(shape, BF16)] * 2
        scratch = (
            twice((2, nblk, HEAD, HEAD))
            + twice((nx, long_in, HEAD)) + twice((nx, long_in, HEAD))
            + twice((nx, long_out, HEAD)) + twice((nx, long_out, HEAD))
            + [pltpu.VMEM((slots + 1, HEAD, HEAD), F32)] * 2
            + twice((2, nblk, HEAD, HEAD))
            + twice((2, 2, PLANE // 2, HEAD, HEAD))
            + twice((2, max(far - 1, 1), 2, PLANE, HEAD, HEAD))
            + twice((2, PLANE, HEAD, HEAD))
            + [pltpu.VMEM((nx, SPAN, HEAD), F32)] * 2
            + [pltpu.VMEM((nx, 8, HEAD), jnp.int32)] * 2 + [pltpu.VMEM((8, HEAD), jnp.int32)]
            + [pltpu.SMEM((nx, 8, HEAD), jnp.int32)] * 2 + [pltpu.SMEM((8, HEAD), jnp.int32)]
            + [sem, sem((3,)), sem((6,)), sem((7,))] + [sem((2, 2, far, 2))] * 4
            + [sem((6,)), sem((3,))]
        )
        hbm = pl.BlockSpec(memory_space=pl.ANY)
        out = pl.pallas_call(
            functools.partial(kernel, nz, nx),
            out_shape=(
                jax.ShapeDtypeStruct(queries.shape, BF16),
                jax.ShapeDtypeStruct(queries.shape, BF16),
                jax.ShapeDtypeStruct(keys_values.shape, BF16),
            ),
            in_specs=[hbm, hbm, hbm, hbm],
            out_specs=(hbm, hbm, hbm),
            scratch_shapes=scratch,
            compiler_params=pltpu.CompilerParams(
                collective_id=0, has_side_effects=True, vmem_limit_bytes=60 * 1024 * 1024
            ),
            name="plane_attention",
        )(links, queries, keys_values, grad_context)
        return tuple(results(*out))

    in_specs = (
        P("grp", "seq", None),
        P(None, "seq", "grp", None),
        P("grp", None, None),
        P("grp", "seq", None),
    )
    out_specs = (P("grp", "seq", None), P("grp", "seq", None), P(None, "seq", "grp", None))
    return jax.shard_map(step, mesh=mesh, in_specs=in_specs, out_specs=out_specs, check_vma=False)
```
